512 devices in a mesh: ctx: 64 (over z, y), head: 8 (over x, core).
Axes of the slice: x: 4, y: 8, z: 8, core: 2. Of those that a mesh axis runs over, the one named last changes fastest.
Arguments:
- queries: bfloat16 [512, 8192], P('ctx', 'head'), may hold values from -6 to 6
- cache_keys: bfloat16 [65536, 8, 128], P('ctx', 'head'), may hold values from -6 to 6
- cache_values: bfloat16 [65536, 8, 128], P('ctx', 'head'), may hold values from -6 to 6
- vertical_blocks: int32 [64, 8], P('head'), may hold values from 0 to 511, as said below
- slash_offsets: int32 [64, 48], P('head'), may hold values from 0 to 511, as said below
- out_weight: bfloat16 [8192, 8192], P('head', 'ctx'), may hold values from -0.0625 to 0.0625
Outputs:
- projected: bfloat16 [512, 8192], P('head', 'ctx')
The draws below stay inside these ranges and needn't reach their ends.
Inputs may be any that keep to these rules, and one draw needn't show every extreme that they name: `vertical_blocks`: every head's list holds block 0; entries may repeat, and a block counts once however often it is named. `slash_offsets`: every head's list holds offset 0; entries may repeat, and a block counts once however often it is reached.
All inputs are finite; a program needn't handle non-finite values.
Results may differ from the reference program's by a relative error of at most 0.007.
Values may be sent and summed in bfloat16 or wider, within the bound.
A program may use at most 64 MiB of HBM per device.

```python
from functools import partial
import jax
import jax.numpy as jnp
from jax import lax

D = 8192
HEADS = 64
KV_HEADS = 8
HEAD_DIM = 128
BLOCK = 128
NV = 8
NS = 48
Q_LEN = 512
CTX_DEV = 1024
GROUP = 8
CONTEXT = 65536
KB_ALL = 512
Q_BLOCKS = 4


def draw_queries(key, part):
    noise_key = jax.random.fold_in(key, 1)
    shape_four = (Q_LEN, KV_HEADS, GROUP, HEAD_DIM)
    drawn = jnp.clip(jax.random.normal(noise_key, shape_four, dtype=jnp.float32), -4.0, 4.0)
    return drawn.reshape(Q_LEN, HEADS * HEAD_DIM).astype(jnp.bfloat16)


def draw_cache_keys(key, part):
    noise_key = jax.random.fold_in(key, 2)
    shape_three = (CONTEXT, KV_HEADS, HEAD_DIM)
    drawn = jnp.clip(jax.random.normal(noise_key, shape_three, dtype=jnp.float32), -4.0, 4.0)
    return drawn.astype(jnp.bfloat16)


def draw_vertical_blocks(key, part):
    picks = jax.random.randint(jax.random.fold_in(key, 11), (HEADS, NV), 1, KB_ALL)
    which = jax.random.randint(jax.random.fold_in(key, 12), (), 0, HEADS)
    picks = picks.at[:, 0].set(0)
    picks = picks.at[:, 1].set(jnp.where(jnp.arange(HEADS) == which, KB_ALL - 1, picks[:, 1]))
    return picks.astype(jnp.int32)


def draw_slash_offsets(key, part):
    near = jax.random.randint(jax.random.fold_in(key, 13), (HEADS, NS), 0, 2 * CTX_DEV // BLOCK)
    far = jax.random.randint(jax.random.fold_in(key, 14), (HEADS, NS), 0, KB_ALL)
    coin = jax.random.randint(jax.random.fold_in(key, 15), (HEADS, NS), 0, 4)
    picks = jnp.where(coin == 0, far, near)
    which = jax.random.randint(jax.random.fold_in(key, 16), (), 0, HEADS)
    picks = picks.at[:, 0].set(0)
    picks = picks.at[:, 1].set(jnp.where(jnp.arange(HEADS) == which, KB_ALL - 1, picks[:, 1]))
    return picks.astype(jnp.int32)


def shard_levels(rng, extent, shards, smallest, high):
    loudness, own = 1.0, jax.random.fold_in(rng, 6)
    for dim, blocks in shards:
        steps = jnp.exp(jax.random.uniform(jax.random.fold_in(own, dim), (blocks,), jnp.float32, smallest / len(shards), high / len(shards)))
        loudness = loudness * jnp.repeat(steps, extent[dim] // blocks).reshape([-1 if axis == dim else 1 for axis in range(len(extent))])
    return loudness


def gaussian(key, shape, spread, bound, pieces=(), kind=jnp.bfloat16):
    gain = shard_levels(key, shape, pieces, -0.22, 0.18) if pieces else 1.0
    result = jax.random.normal(key, shape, jnp.float32) * spread * gain
    return jnp.minimum(jnp.maximum(result, -bound), bound).astype(kind)


def setup_inputs(seed: int = 0) -> dict:
    seeds = jax.random.split(jax.random.key(seed), 7)
    return {
        "queries": draw_queries(jax.random.fold_in(seeds[6], 71), 0),
        "cache_keys": draw_cache_keys(jax.random.fold_in(seeds[6], 71), 0),
        "cache_values": gaussian(seeds[2], (CONTEXT, KV_HEADS, HEAD_DIM), 1.0, 6.0, ((0, 64), (1, 8))),
        "vertical_blocks": draw_vertical_blocks(jax.random.fold_in(seeds[6], 71), 0),
        "slash_offsets": draw_slash_offsets(jax.random.fold_in(seeds[6], 71), 0),
        "out_weight": gaussian(seeds[5], (HEADS * HEAD_DIM, D), (HEADS * HEAD_DIM) ** -0.5, 0.0625, ((0, 8), (1, 64))),
    }


NEG_FILL = -1e30


def head_rows(head_index, queries, cache_keys, cache_values, vertical_blocks, slash_offsets):
    group_index = head_index // GROUP
    key_rows = lax.dynamic_index_in_dim(cache_keys, group_index, 1, keepdims=False).reshape(KB_ALL, BLOCK, HEAD_DIM)
    value_rows = lax.dynamic_index_in_dim(cache_values, group_index, 1, keepdims=False).reshape(KB_ALL, BLOCK, HEAD_DIM)
    query_rows = lax.dynamic_index_in_dim(queries.reshape(Q_LEN, HEADS, HEAD_DIM), head_index, 1, keepdims=False)
    vertical_row = lax.dynamic_index_in_dim(vertical_blocks, head_index, 0, keepdims=False)
    slash_row = lax.dynamic_index_in_dim(slash_offsets, head_index, 0, keepdims=False)
    position = jnp.arange(NV + NS, dtype=jnp.int32)

    def query_block(block_index):
        global_block = KB_ALL - Q_BLOCKS + block_index
        candidates = jnp.concatenate([vertical_row.astype(jnp.int32), (global_block - slash_row).astype(jnp.int32)])
        earlier = (candidates[:, None] == candidates[None, :]) & (position[None, :] < position[:, None])
        usable = (candidates >= 0) & jnp.logical_not(jnp.any(earlier, axis=1))
        clipped = jnp.clip(candidates, 0, KB_ALL - 1).astype(jnp.int32)
        key_tiles = key_rows[clipped].astype(jnp.float32)
        value_tiles = value_rows[clipped].astype(jnp.float32)
        query_tile = lax.dynamic_slice_in_dim(query_rows, (block_index * BLOCK).astype(jnp.int32), BLOCK, 0).astype(jnp.float32)
        scores = jnp.einsum("qd,ckd->qck", query_tile, key_tiles, precision=lax.Precision.HIGHEST) * (HEAD_DIM ** -0.5)
        key_pos = clipped[:, None] * BLOCK + jnp.arange(BLOCK, dtype=jnp.int32)[None, :]
        query_pos = CONTEXT - Q_LEN + block_index * BLOCK + jnp.arange(BLOCK, dtype=jnp.int32)
        allowed_mask = usable[None, :, None] & (key_pos[None, :, :] <= query_pos[:, None, None])
        masked = jnp.where(allowed_mask, scores, NEG_FILL)
        block_peak = jnp.max(masked, axis=-1)
        safe_peak = jnp.where(block_peak > 0.5 * NEG_FILL, block_peak, 0.0)
        weights = jnp.where(allowed_mask, jnp.exp(scores - safe_peak[..., None]), 0.0).astype(jnp.bfloat16)
        weights_wide = weights.astype(jnp.float32)
        block_total = jnp.sum(weights_wide, axis=-1)
        block_out = jnp.einsum("qck,ckd->qcd", weights_wide, value_tiles, precision=lax.Precision.HIGHEST)
        row_peak = jnp.max(block_peak, axis=1)
        factor = jnp.exp(block_peak - row_peak[:, None])
        numer = jnp.sum(factor[..., None] * block_out, axis=1)
        denom = jnp.sum(factor * block_total, axis=1)
        return numer / denom[:, None]

    tiles = lax.map(query_block, jnp.arange(Q_BLOCKS, dtype=jnp.int32))
    return tiles.reshape(Q_LEN, HEAD_DIM)


def reference(queries, cache_keys, cache_values, vertical_blocks, slash_offsets, out_weight):
    one_head = partial(head_rows, queries=queries, cache_keys=cache_keys, cache_values=cache_values,
                       vertical_blocks=vertical_blocks, slash_offsets=slash_offsets)
    per_head = lax.map(one_head, jnp.arange(HEADS, dtype=jnp.int32))
    attention = jnp.transpose(per_head, (1, 0, 2)).reshape(Q_LEN, HEADS * HEAD_DIM).astype(jnp.bfloat16)
    return jnp.dot(attention, out_weight, preferred_element_type=jnp.float32).astype(jnp.bfloat16)
```

```python
import functools
import math

import jax
import jax.numpy as jnp
from jax import lax
from jax.experimental import pallas as pl
from jax.experimental.pallas import tpu as pltpu
from jax.sharding import PartitionSpec as P

MESH = pl.DeviceIdType.MESH
BF16, F32 = jnp.bfloat16, jnp.float32
NEG = -1e30
R = 8
ORDER = (4, 3, 5, 2, 6, 1, 7)
GROUPS = 2
NH = 4 // GROUPS
KINDS = (0, 1)
ROWS1 = NH * 64 + 16
PIECE = NH * 8
PARTS = 64 // PIECE
ROWS2 = PIECE + 16


def dot(a, b):
    return jnp.dot(a, b, preferred_element_type=F32)


def pack_stats(top, low, rest):
    return jnp.concatenate([jnp.where(lax.broadcasted_iota(jnp.int32, (8, 128), 1) < 64, top, low), rest], 0)


def split3(x):
    hi = x.astype(BF16).astype(F32)
    mid = (x - hi).astype(BF16).astype(F32)
    return hi, mid, (x - hi) - mid


def unpack_stats(block):
    block = block.astype(F32)
    first = block[:8]
    other = pltpu.roll(first, 64, 1)
    lane = lax.broadcasted_iota(jnp.int32, (8, 128), 1)
    hi = jnp.where(lane < 64, first, other)
    mid = jnp.where(lane < 64, other, first)
    return hi + (mid + block[8:])


def kernel(
    q_ref, k_hbm, v_hbm, vert_ref, slash_ref, w_hbm, o_ref,
    k_in, v_ext, w_ref, kt, bias, tri, qbuf, stat,
    snd1, rcv1, snd2, rcv2, wcol, attn, proj, snd3, rcv3,
    load_sem, send_sem, recv_sem,
):
    ctx, hd = lax.axis_index("ctx"), lax.axis_index("head")
    z, y = ctx // R, ctx % R
    heads = q_ref.shape[1] // 128

    def along(axis, k):
        return {"ctx": z * R + (y + k) % R} if axis == 0 else {"ctx": (z + k) % R * R + y}

    def place(axis):
        return y if axis == 0 else z

    barrier = pltpu.get_barrier_semaphore()
    for k in ORDER:
        for axis in (0, 1):
            pl.semaphore_signal(barrier, inc=1, device_id=along(axis, k), device_id_type=MESH)
        pl.semaphore_signal(barrier, inc=1, device_id={"head": (hd + k) % R}, device_id_type=MESH)

    loads = [
        pltpu.make_async_copy(k_hbm, k_in, load_sem.at[0]),
        pltpu.make_async_copy(v_hbm, v_ext.at[:, pl.ds(0, 128)], load_sem.at[1]),
        pltpu.make_async_copy(w_hbm, w_ref, load_sem.at[2]),
    ]
    for copy in loads:
        copy.start()
    for h in range(heads):
        qbuf[h, z, y] = q_ref[:, h * 128 : (h + 1) * 128]

    pl.semaphore_wait(barrier, 3 * (R - 1))

    def send(src, dst, slot, device):
        copy = pltpu.make_async_remote_copy(
            src_ref=src, dst_ref=dst, send_sem=send_sem.at[slot], recv_sem=recv_sem.at[slot],
            device_id=device, device_id_type=MESH,
        )
        copy.start()

    pending = []

    def arrived(like, slot):
        copy = pltpu.make_async_remote_copy(
            src_ref=like, dst_ref=like, send_sem=send_sem.at[slot], recv_sem=recv_sem.at[slot],
            device_id=along(0, 1), device_id_type=MESH,
        )
        copy.wait_recv()
        pending.append(copy)

    def slot(phase, kind, group):
        return (phase * 2 + kind) * GROUPS + group

    def head_span(kind, group):
        return pl.ds(kind * 4 + group * NH, NH)

    def q1_send(group):
        for k in ORDER:
            for kind in KINDS:
                ref = qbuf.at[head_span(kind, group), z, y]
                send(ref, ref, slot(0, kind, group), along(kind, k))

    def q1_wait(group):
        for kind in KINDS:
            arrived(qbuf.at[head_span(kind, group), 0, pl.ds(0, R - 1)], slot(0, kind, group))

    def q2_send(group):
        for k in ORDER:
            for kind in KINDS:
                span = head_span(kind, group)
                ref = qbuf.at[span, z] if kind == 0 else qbuf.at[span, :, y]
                send(ref, ref, slot(1, kind, group), along(1 - kind, k))

    def q2_wait(group):
        for kind in KINDS:
            arrived(qbuf.at[head_span(kind, group), pl.ds(0, R - 1)], slot(1, kind, group))

    lane = lax.broadcasted_iota(jnp.int32, (8, 128), 1)
    sub = lax.broadcasted_iota(jnp.int32, (8, 128), 0)
    scale = math.log2(math.e) / math.sqrt(128.0)

    def prepare():
        first = 508 - 8 * ctx
        vert, slash = vert_ref[...], slash_ref[...]
        by_slash = {
            d: jnp.max(jnp.where(slash == first + d, 1.0, 0.0), axis=1, keepdims=True) for d in range(-7, 4)
        }
        by_vert = [jnp.max(jnp.where(vert == 8 * ctx + j, 1.0, 0.0), axis=1, keepdims=True) for j in range(8)]
        for b in range(4):
            for j in range(8):
                hit = jnp.maximum(by_slash[b - j], by_vert[j])
                row = jnp.broadcast_to(jnp.where(hit > 0.5, 0.0, NEG), (heads, 128))
                if j > b + 4:
                    row = jnp.where(ctx == R * R - 1, NEG, row)
                bias[:, b, j * 128 : (j + 1) * 128] = row
        r128 = lax.broadcasted_iota(jnp.int32, (128, 128), 0)
        c128 = lax.broadcasted_iota(jnp.int32, (128, 128), 1)
        tri[...] = jnp.where((c128 <= r128) | (ctx != R * R - 1), 0.0, NEG)
        v_ext[:, 128:] = jnp.ones((v_ext.shape[0], 128), BF16)
        stat[...] = jnp.zeros_like(stat)
        for copy in loads:
            copy.wait()
        kt[...] = k_in[...].astype(F32).T.astype(BF16)

    def attend(kind, group):
        def one_head(hh, _):
            h = kind * 4 + group * NH + hh
            limits = bias[h]
            for b in range(4):
                q = qbuf[h, 2 * b : 2 * b + 2].reshape(128, 128)
                s = dot(q, kt[...]) * scale + limits[b : b + 1, :]
                c = (4 + b) * 128
                diag = s[:, c : c + 128] + tri[...]
                parts = [s[:, :c], diag] + ([s[:, c + 128 :]] if b < 3 else [])
                s = jnp.concatenate(parts, axis=1)
                m = jnp.max(s, axis=1, keepdims=True)
                p = jnp.exp2(s - m).astype(BF16)
                out = dot(p, v_ext[...])
                total = out[:, 128:]
                mean = (out[:, :128] / total).astype(BF16)
                snd1[kind, group, 2 * b : 2 * b + 2, pl.ds(pl.multiple_of(hh * 64, 64), 64), :] = mean.reshape(2, 64, 128)
                lse = m + jnp.log2(total)
                rows = slice(b * 128, (b + 1) * 128)
                at = lax.broadcasted_iota(jnp.int32, (128, 128), 1)
                stat[rows, :] = jnp.where(at == hh, lse, stat[rows, :])
            return 0

        lax.fori_loop(0, NH, one_head, 0)
        for b in range(4):
            block = stat[b * 128 : (b + 1) * 128, :].T[:8]
            hi, mid, lo = split3(block)
            turned = [pltpu.roll(x, 64, 1) for x in (hi, mid, lo)]
            even = pack_stats(hi, turned[1], jnp.where(lane < 64, lo, turned[2]))
            odd = pack_stats(turned[0], mid, jnp.where(lane < 64, turned[2], lo))
            snd1[kind, group, 2 * b, NH * 64 :, :] = even.astype(BF16)
            snd1[kind, group, 2 * b + 1, NH * 64 :, :] = odd.astype(BF16)

    def r1_send(kind, group):
        for k in ORDER:
            to = (place(kind) + k) % R
            send(snd1.at[kind, group, to], rcv1.at[kind, group, k - 1], slot(2, kind, group), along(kind, k))

    def r1_combine(kind, group):
        arrived(rcv1.at[kind, group], slot(2, kind, group))
        own = snd1.at[kind, group, place(kind)]
        refs = [own] + [rcv1.at[kind, group, k] for k in range(R - 1)]
        logs = [unpack_stats(ref[NH * 64 :, :]) for ref in refs]
        top = functools.reduce(jnp.maximum, logs)
        raised = [jnp.exp2(x - top) for x in logs]
        total = functools.reduce(jnp.add, raised)
        cols = jnp.concatenate([x / total for x in raised] + [jnp.zeros((64, 128), F32)], 0).T
        for hh in range(NH):
            acc = None
            for s, ref in enumerate(refs):
                term = cols[:64, s * 8 + hh : s * 8 + hh + 1] * ref[hh * 64 : (hh + 1) * 64, :].astype(F32)
                acc = term if acc is None else acc + term
            acc = acc.astype(BF16).reshape(PARTS, PIECE, 128)
            snd2[kind, group, hh * PARTS : (hh + 1) * PARTS, :PIECE, :] = acc
        hi, mid, lo = split3(top + jnp.log2(total))
        packed = pack_stats(hi, mid, lo).astype(BF16)
        for to in range(R):
            snd2[kind, group, to, PIECE:, :] = packed

    def r2_send(kind, group):
        axis = 1 - kind
        for k in ORDER:
            to = (place(axis) + k) % R
            send(snd2.at[kind, group, to], rcv2.at[kind, group, k - 1], slot(3, kind, group), along(axis, k))

    def own_piece(kind, group):
        axis = 1 - kind
        me = place(axis)
        start = pl.multiple_of(me % PARTS * PIECE, PIECE)
        return attn.at[kind, group, place(kind), me // PARTS, pl.ds(start, PIECE)]

    def r2_combine(kind, group):
        arrived(rcv2.at[kind, group], slot(3, kind, group))
        me = place(1 - kind)
        hh, part = me // PARTS, me % PARTS
        refs = [snd2.at[kind, group, me]] + [rcv2.at[kind, group, k] for k in range(R - 1)]
        logs = jnp.zeros((8, 128), F32)
        for s, ref in enumerate(refs):
            row = jnp.sum(jnp.where(sub == hh, unpack_stats(ref[PIECE:, :]), 0.0), axis=0, keepdims=True)
            logs = jnp.where(sub == s, row, logs)
        raised = jnp.exp2(logs - jnp.max(logs, axis=0, keepdims=True))
        weight = raised / jnp.sum(raised, axis=0, keepdims=True)
        wcol[...] = jnp.concatenate([weight, jnp.zeros((120, 128), F32)], 0).T
        cols = wcol[pl.ds(pl.multiple_of(part * PIECE, PIECE), PIECE), :]
        acc = None
        for s, ref in enumerate(refs):
            term = cols[:, s : s + 1] * ref[:PIECE, :].astype(F32)
            acc = term if acc is None else acc + term
        own_piece(kind, group)[...] = acc.astype(BF16)

    def g1_send(kind, group):
        for k in ORDER:
            ref = own_piece(kind, group)
            send(ref, ref, slot(4, kind, group), along(1 - kind, k))

    def g1_wait(kind, group):
        arrived(rcv2.at[kind, group, :, pl.ds(0, PIECE)], slot(4, kind, group))

    def g2_send(kind, group):
        ref = attn.at[kind, group, place(kind)]
        for k in ORDER:
            send(ref, ref, slot(5, kind, group), along(kind, k))

    def g2_wait(kind, group):
        arrived(attn.at[kind, group, pl.ds(0, R - 1)], slot(5, kind, group))

    def project(kind, group):
        acc = None
        for hh in range(0, NH, 2):
            left = [attn[kind, group, :, hh + i].reshape(512, 128) for i in range(2)]
            row = (kind * 4 + group * NH + hh) * 128
            term = dot(jnp.concatenate(left, 1), w_ref[row : row + 256, :])
            acc = term if acc is None else acc + term
        return acc

    every = [(kind, group) for group in range(GROUPS) for kind in KINDS]
    for group in range(GROUPS):
        q1_send(group)
    prepare()
    for group in range(GROUPS):
        q1_wait(group)
        q2_send(group)
    for group in range(GROUPS):
        q2_wait(group)
        for kind in KINDS:
            attend(kind, group)
            r1_send(kind, group)
    for group in range(GROUPS):
        for kind in KINDS:
            r1_combine(kind, group)
            r2_send(kind, group)
        for kind in KINDS:
            r2_combine(kind, group)
            g1_send(kind, group)
        if group:
            for kind in KINDS:
                g1_wait(kind, group - 1)
                g2_send(kind, group - 1)
    for kind in KINDS:
        g1_wait(kind, GROUPS - 1)
        g2_send(kind, GROUPS - 1)
    total = None
    for kind, group in every:
        g2_wait(kind, group)
        term = project(kind, group)
        total = term if total is None else total + term
    proj[...] = total
    snd3[...] = total.astype(BF16).reshape(R, 64, 128)
    last = slot(6, 0, 0)
    for k in ORDER:
        to = (hd + k) % R
        send(snd3.at[to], rcv3.at[k - 1], last, {"head": to})
    arrived(rcv3, last)
    out = proj[pl.ds(pl.multiple_of(hd * 64, 64), 64), :]
    for k in range(R - 1):
        out = out + rcv3[k].astype(F32)
    o_ref[...] = out.astype(BF16)
    for copy in pending:
        copy.wait_send()


def body(queries, cache_keys, cache_values, vertical_blocks, slash_offsets, out_weight):
    keys, values = cache_keys[:, 0, :], cache_values[:, 0, :]
    local, width = keys.shape
    heads = vertical_blocks.shape[0]
    slots = 6 * 2 * GROUPS + 1
    vmem, hbm = pl.BlockSpec(memory_space=pltpu.VMEM), pl.BlockSpec(memory_space=pl.ANY)
    return pl.pallas_call(
        kernel,
        out_shape=jax.ShapeDtypeStruct((64, 128), BF16),
        in_specs=[vmem, hbm, hbm, vmem, vmem, hbm],
        out_specs=vmem,
        scratch_shapes=[
            pltpu.VMEM((local, width), BF16),
            pltpu.VMEM((local, 256), BF16),
            pltpu.VMEM(out_weight.shape, BF16),
            pltpu.VMEM((width, local), BF16),
            pltpu.VMEM((heads, 4, local), F32),
            pltpu.VMEM((128, 128), F32),
            pltpu.VMEM((heads, R, R, 8, 128), BF16),
            pltpu.VMEM((512, 128), F32),
            pltpu.VMEM((2, GROUPS, R, ROWS1, 128), BF16),
            pltpu.VMEM((2, GROUPS, R - 1, ROWS1, 128), BF16),
            pltpu.VMEM((2, GROUPS, R, ROWS2, 128), BF16),
            pltpu.VMEM((2, GROUPS, R - 1, ROWS2, 128), BF16),
            pltpu.VMEM((128, 128), F32),
            pltpu.VMEM((2, GROUPS, R, NH, 64, 128), BF16),
            pltpu.VMEM((512, 128), F32),
            pltpu.VMEM((R, 64, 128), BF16),
            pltpu.VMEM((R - 1, 64, 128), BF16),
            pltpu.SemaphoreType.DMA((3,)),
            pltpu.SemaphoreType.DMA((slots,)),
            pltpu.SemaphoreType.DMA((slots,)),
        ],
        compiler_params=pltpu.CompilerParams(
            collective_id=0, has_side_effects=True, vmem_limit_bytes=48 * 1024 * 1024
        ),
    )(queries, keys, values, vertical_blocks, slash_offsets, out_weight)


def solution(mesh):
    return jax.shard_map(
        body,
        mesh=mesh,
        in_specs=(
            P("ctx", "head"),
            P("ctx", "head", None),
            P("ctx", "head", None),
            P("head", None),
            P("head", None),
            P("head", "ctx"),
        ),
        out_specs=P("head", "ctx"),
        check_vma=False,
    )
```

```python
import functools
import math

import jax
import jax.numpy as jnp
from jax import lax
from jax.experimental import pallas as pl
from jax.experimental.pallas import tpu as pltpu
from jax.sharding import PartitionSpec as P

MESH = pl.DeviceIdType.MESH
BF16, F32 = jnp.bfloat16, jnp.float32
NEG = -1e30
R = 8
ORDER = (4, 3, 5, 2, 6, 1, 7)
GROUPS = 2
NH = 4 // GROUPS
KINDS = (0, 1)
ROWS1 = NH * 64 + 16
PIECE = NH * 8
PARTS = 64 // PIECE
ROWS2 = PIECE + 16


def dot(a, b):
    return jnp.dot(a, b, preferred_element_type=F32)


def pack_stats(top, low, rest):
    return jnp.concatenate([jnp.where(lax.broadcasted_iota(jnp.int32, (8, 128), 1) < 64, top, low), rest], 0)


def split3(x):
    hi = x.astype(BF16).astype(F32)
    mid = (x - hi).astype(BF16).astype(F32)
    return hi, mid, (x - hi) - mid


def unpack_stats(block):
    block = block.astype(F32)
    first = block[:8]
    other = pltpu.roll(first, 64, 1)
    lane = lax.broadcasted_iota(jnp.int32, (8, 128), 1)
    hi = jnp.where(lane < 64, first, other)
    mid = jnp.where(lane < 64, other, first)
    return hi + (mid + block[8:])


def kernel(
    q_hbm, k_hbm, v_hbm, vert_hbm, slash_hbm, w_hbm, o_ref,
    q_in, vert_in, slash_in, k_in, v_ext, w_ref, ktx, tri, qbuf, score, prob, stat,
    snd1, rcv1, snd2, rcv2, wcol, attn, proj, snd3, rcv3,
    load_sem, send_sem, recv_sem,
):
    ctx, hd = lax.axis_index("ctx"), lax.axis_index("head")
    z, y = ctx // R, ctx % R
    heads = q_in.shape[1] // 128

    def along(axis, k):
        return {"ctx": z * R + (y + k) % R} if axis == 0 else {"ctx": (z + k) % R * R + y}

    def place(axis):
        return y if axis == 0 else z

    loads = [
        pltpu.make_async_copy(src, dst, load_sem.at[i])
        for i, (src, dst) in enumerate(
            [
                (q_hbm, q_in),
                (vert_hbm, vert_in),
                (slash_hbm, slash_in),
                (k_hbm, k_in),
                (v_hbm, v_ext.at[:, pl.ds(0, 128)]),
                (w_hbm, w_ref),
            ]
        )
    ]
    for copy in loads:
        copy.start()
    barrier = pltpu.get_barrier_semaphore()
    for k in ORDER:
        for axis in (0, 1):
            pl.semaphore_signal(barrier, inc=1, device_id=along(axis, k), device_id_type=MESH)
        pl.semaphore_signal(barrier, inc=1, device_id={"head": (hd + k) % R}, device_id_type=MESH)

    loads[0].wait()
    for h in range(heads):
        qbuf[h, z, y] = q_in[:, h * 128 : (h + 1) * 128]

    pl.semaphore_wait(barrier, 3 * (R - 1))

    def send(src, dst, slot, device):
        copy = pltpu.make_async_remote_copy(
            src_ref=src, dst_ref=dst, send_sem=send_sem.at[slot], recv_sem=recv_sem.at[slot],
            device_id=device, device_id_type=MESH,
        )
        copy.start()

    pending = []

    def arrived(like, slot):
        copy = pltpu.make_async_remote_copy(
            src_ref=like, dst_ref=like, send_sem=send_sem.at[slot], recv_sem=recv_sem.at[slot],
            device_id=along(0, 1), device_id_type=MESH,
        )
        copy.wait_recv()
        pending.append(copy)

    def slot(phase, kind, group):
        return (phase * 2 + kind) * 4 + group

    def q1_send():
        for k in ORDER:
            for kind in KINDS:
                ref = qbuf.at[pl.ds(4 * kind, 4), z, y]
                send(ref, ref, slot(0, kind, 0), along(kind, k))

    def q1_wait():
        for kind in KINDS:
            arrived(qbuf.at[pl.ds(4 * kind, 4), 0, pl.ds(0, R - 1)], slot(0, kind, 0))

    def q2_send(pair):
        for k in ORDER:
            for kind in KINDS:
                h = 4 * kind + pair
                ref = qbuf.at[h, z] if kind == 0 else qbuf.at[h, :, y]
                send(ref, ref, slot(1, kind, pair), along(1 - kind, k))

    def q2_wait(pair):
        for kind in KINDS:
            arrived(qbuf.at[4 * kind + pair, pl.ds(0, R - 1)], slot(1, kind, pair))

    lane = lax.broadcasted_iota(jnp.int32, (8, 128), 1)
    sub = lax.broadcasted_iota(jnp.int32, (8, 128), 0)
    scale = math.log2(math.e) / math.sqrt(128.0)

    def prepare():
        for copy in loads[1:]:
            copy.wait()
        v_ext[:, 128:] = jnp.ones((v_ext.shape[0], 128), BF16)
        stat[...] = jnp.zeros_like(stat)
        kt = k_in[...].astype(F32).T.astype(BF16)
        for h in range(heads):
            ktx[h, :128, :] = kt

    def prepare_masks():
        first = 508 - 8 * ctx
        vert, slash = vert_in[...], slash_in[...]
        by_slash = {
            d: jnp.max(jnp.where(slash == first + d, 1.0, 0.0), axis=1, keepdims=True) for d in range(-7, 4)
        }
        by_vert = [jnp.max(jnp.where(vert == 8 * ctx + j, 1.0, 0.0), axis=1, keepdims=True) for j in range(8)]
        masks = []
        for b in range(4):
            blocks = []
            for j in range(8):
                hit = jnp.maximum(by_slash[b - j], by_vert[j])
                row = jnp.broadcast_to(jnp.where(hit > 0.5, 0.0, NEG), (heads, 128))
                if j > b + 4:
                    row = jnp.where(ctx == R * R - 1, NEG, row)
                blocks.append(row)
            masks.append(jnp.concatenate(blocks, 1))
        local = masks[0].shape[1]
        for h in range(heads):
            rows = [mask[h : h + 1, :] for mask in masks] + [jnp.zeros((124, local), F32)]
            ktx[h, 128:, :] = jnp.concatenate(rows, 0).astype(BF16)
        r128 = lax.broadcasted_iota(jnp.int32, (128, 128), 0)
        c128 = lax.broadcasted_iota(jnp.int32, (128, 128), 1)
        tri[...] = jnp.where((c128 <= r128) | (ctx != R * R - 1), 0.0, NEG)

    def scores(kind, pair):
        row = lax.broadcasted_iota(jnp.int32, (512, 128), 0) // 128
        chooser = jnp.where(lax.broadcasted_iota(jnp.int32, (512, 128), 1) == row, 1.0, 0.0).astype(BF16)
        h = 4 * kind + pair
        score[kind] = dot(jnp.concatenate([qbuf[h].reshape(512, 128), chooser], 1), ktx[h])

    def weigh(kind):
        tops = []
        for b in range(4):
            rows = slice(b * 128, (b + 1) * 128)
            c = (4 + b) * 128
            s = score[kind, rows]
            parts = [s[:, :c], s[:, c : c + 128] + tri[...]] + ([s[:, c + 128 :]] if b < 3 else [])
            s = jnp.concatenate(parts, axis=1)
            top = jnp.max(s, axis=1, keepdims=True) * scale
            prob[kind, rows] = jnp.exp2(s * scale - top).astype(BF16)
            tops.append(top)
        return tops

    def finish(kind, pair, tops):
        group, hh = pair // NH, pair % NH
        for b in range(4):
            rows = slice(b * 128, (b + 1) * 128)
            out = dot(prob[kind, rows], v_ext[...])
            total = out[:, 128:]
            mean = (out[:, :128] / total).astype(BF16)
            snd1[kind, group, 2 * b : 2 * b + 2, hh * 64 : (hh + 1) * 64, :] = mean.reshape(2, 64, 128)
            at = lax.broadcasted_iota(jnp.int32, (128, 128), 1)
            stat[kind, rows] = jnp.where(at == hh, tops[b] + jnp.log2(total), stat[kind, rows])

    def attend(pair):
        scores(0, pair)
        tops0 = weigh(0)
        scores(1, pair)
        finish(0, pair, tops0)
        tops1 = weigh(1)
        finish(1, pair, tops1)

    def statistics(kind, group):
        for b in range(4):
            block = stat[kind, b * 128 : (b + 1) * 128, :].T[:8]
            hi, mid, lo = split3(block)
            turned = [pltpu.roll(x, 64, 1) for x in (hi, mid, lo)]
            even = pack_stats(hi, turned[1], jnp.where(lane < 64, lo, turned[2]))
            odd = pack_stats(turned[0], mid, jnp.where(lane < 64, turned[2], lo))
            snd1[kind, group, 2 * b, NH * 64 :, :] = even.astype(BF16)
            snd1[kind, group, 2 * b + 1, NH * 64 :, :] = odd.astype(BF16)

    def r1_send(kind, group):
        for k in ORDER:
            to = (place(kind) + k) % R
            send(snd1.at[kind, group, to], rcv1.at[kind, group, k - 1], slot(2, kind, group), along(kind, k))

    def r1_combine(kind, group):
        arrived(rcv1.at[kind, group], slot(2, kind, group))
        own = snd1.at[kind, group, place(kind)]
        refs = [own] + [rcv1.at[kind, group, k] for k in range(R - 1)]
        logs = [unpack_stats(ref[NH * 64 :, :]) for ref in refs]
        top = functools.reduce(jnp.maximum, logs)
        raised = [jnp.exp2(x - top) for x in logs]
        total = functools.reduce(jnp.add, raised)
        cols = jnp.concatenate([x / total for x in raised] + [jnp.zeros((64, 128), F32)], 0).T
        for hh in range(NH):
            acc = None
            for s, ref in enumerate(refs):
                term = cols[:64, s * 8 + hh : s * 8 + hh + 1] * ref[hh * 64 : (hh + 1) * 64, :].astype(F32)
                acc = term if acc is None else acc + term
            acc = acc.astype(BF16).reshape(PARTS, PIECE, 128)
            snd2[kind, group, hh * PARTS : (hh + 1) * PARTS, :PIECE, :] = acc
        hi, mid, lo = split3(top + jnp.log2(total))
        packed = pack_stats(hi, mid, lo).astype(BF16)
        for to in range(R):
            snd2[kind, group, to, PIECE:, :] = packed

    def r2_send(kind, group):
        axis = 1 - kind
        for k in ORDER:
            to = (place(axis) + k) % R
            send(snd2.at[kind, group, to], rcv2.at[kind, group, k - 1], slot(3, kind, group), along(axis, k))

    def own_piece(kind, group):
        axis = 1 - kind
        me = place(axis)
        start = pl.multiple_of(me % PARTS * PIECE, PIECE)
        return attn.at[kind, group, place(kind), me // PARTS, pl.ds(start, PIECE)]

    def r2_combine(kind, group):
        arrived(rcv2.at[kind, group], slot(3, kind, group))
        me = place(1 - kind)
        hh, part = me // PARTS, me % PARTS
        refs = [snd2.at[kind, group, me]] + [rcv2.at[kind, group, k] for k in range(R - 1)]
        logs = jnp.zeros((8, 128), F32)
        for s, ref in enumerate(refs):
            row = jnp.sum(jnp.where(sub == hh, unpack_stats(ref[PIECE:, :]), 0.0), axis=0, keepdims=True)
            logs = jnp.where(sub == s, row, logs)
        raised = jnp.exp2(logs - jnp.max(logs, axis=0, keepdims=True))
        weight = raised / jnp.sum(raised, axis=0, keepdims=True)
        wcol[...] = jnp.concatenate([weight, jnp.zeros((120, 128), F32)], 0).T
        cols = wcol[pl.ds(pl.multiple_of(part * PIECE, PIECE), PIECE), :]
        acc = None
        for s, ref in enumerate(refs):
            term = cols[:, s : s + 1] * ref[:PIECE, :].astype(F32)
            acc = term if acc is None else acc + term
        own_piece(kind, group)[...] = acc.astype(BF16)

    def g1_send(kind, group):
        for k in ORDER:
            ref = own_piece(kind, group)
            send(ref, ref, slot(4, kind, group), along(1 - kind, k))

    def g1_wait(kind, group):
        arrived(rcv2.at[kind, group, :, pl.ds(0, PIECE)], slot(4, kind, group))

    def g2_send(kind, group):
        ref = attn.at[kind, group, place(kind)]
        for k in ORDER:
            send(ref, ref, slot(5, kind, group), along(kind, k))

    def g2_wait(kind, group):
        arrived(attn.at[kind, group, pl.ds(0, R - 1)], slot(5, kind, group))

    def project(kind, group):
        acc = None
        for hh in range(0, NH, 2):
            left = [attn[kind, group, :, hh + i].reshape(512, 128) for i in range(2)]
            row = (kind * 4 + group * NH + hh) * 128
            term = dot(jnp.concatenate(left, 1), w_ref[row : row + 256, :])
            acc = term if acc is None else acc + term
        return acc

    def tail():
        total = None
        for group in range(GROUPS):
            for kind in KINDS:
                g2_wait(kind, group)
                term = project(kind, group)
                total = term if total is None else total + term
        proj[...] = total
        snd3[...] = total.astype(BF16).reshape(R, 64, 128)
        last = slot(6, 0, 0)
        for k in ORDER:
            to = (hd + k) % R
            send(snd3.at[to], rcv3.at[k - 1], last, {"head": to})
        arrived(rcv3, last)
        out = proj[pl.ds(pl.multiple_of(hd * 64, 64), 64), :]
        for k in range(R - 1):
            out = out + rcv3[k].astype(F32)
        o_ref[...] = out.astype(BF16)

    steps = [(q1_send,), (prepare,), (q1_wait,)]
    steps += [(q2_send, pair) for pair in range(4)] + [(prepare_masks,)]
    for pair in range(4):
        steps += [(q2_wait, pair), (attend, pair)]
        if pair % NH == NH - 1:
            for kind in KINDS:
                steps += [(statistics, kind, pair // NH), (r1_send, kind, pair // NH)]
    both = [(kind, group) for group in range(GROUPS) for kind in KINDS]
    for first, second in ((r1_combine, r2_send), (r2_combine, g1_send), (g1_wait, g2_send)):
        for args in both:
            steps += [(first, *args), (second, *args)]
    steps += [(tail,)]
    for step, *args in steps:
        step(*args)
    for copy in pending:
        copy.wait_send()


def body(queries, cache_keys, cache_values, vertical_blocks, slash_offsets, out_weight):
    keys, values = cache_keys[:, 0, :], cache_values[:, 0, :]
    local, width = keys.shape
    heads = vertical_blocks.shape[0]
    slots = 6 * 2 * 4 + 1
    vmem, hbm = pl.BlockSpec(memory_space=pltpu.VMEM), pl.BlockSpec(memory_space=pltpu.HBM)
    return pl.pallas_call(
        kernel,
        out_shape=jax.ShapeDtypeStruct((64, 128), BF16),
        in_specs=[hbm] * 6,
        out_specs=vmem,
        scratch_shapes=[
            pltpu.VMEM(queries.shape, BF16),
            pltpu.VMEM(vertical_blocks.shape, jnp.int32),
            pltpu.VMEM(slash_offsets.shape, jnp.int32),
            pltpu.VMEM((local, width), BF16),
            pltpu.VMEM((local, 256), BF16),
            pltpu.VMEM(out_weight.shape, BF16),
            pltpu.VMEM((heads, 2 * width, local), BF16),
            pltpu.VMEM((128, 128), F32),
            pltpu.VMEM((heads, R, R, 8, 128), BF16),
            pltpu.VMEM((2, 512, local), F32),
            pltpu.VMEM((2, 512, local), BF16),
            pltpu.VMEM((2, 512, 128), F32),
            pltpu.VMEM((2, GROUPS, R, ROWS1, 128), BF16),
            pltpu.VMEM((2, GROUPS, R - 1, ROWS1, 128), BF16),
            pltpu.VMEM((2, GROUPS, R, ROWS2, 128), BF16),
            pltpu.VMEM((2, GROUPS, R - 1, ROWS2, 128), BF16),
            pltpu.VMEM((128, 128), F32),
            pltpu.VMEM((2, GROUPS, R, NH, 64, 128), BF16),
            pltpu.VMEM((512, 128), F32),
            pltpu.VMEM((R, 64, 128), BF16),
            pltpu.VMEM((R - 1, 64, 128), BF16),
            pltpu.SemaphoreType.DMA((6,)),
            pltpu.SemaphoreType.DMA((slots,)),
            pltpu.SemaphoreType.DMA((slots,)),
        ],
        compiler_params=pltpu.CompilerParams(
            collective_id=0, has_side_effects=True, vmem_limit_bytes=61 * 1024 * 1024
        ),
    )(queries, keys, values, vertical_blocks, slash_offsets, out_weight)


def solution(mesh):
    return jax.shard_map(
        body,
        mesh=mesh,
        in_specs=(
            P("ctx", "head"),
            P("ctx", "head", None),
            P("ctx", "head", None),
            P("head", None),
            P("head", None),
            P("head", "ctx"),
        ),
        out_specs=P("head", "ctx"),
        check_vma=False,
    )
```

```python
import functools
import math

import jax
import jax.numpy as jnp
from jax import lax
from jax.experimental import pallas as pl
from jax.experimental.pallas import tpu as pltpu
from jax.sharding import PartitionSpec as P

MESH = pl.DeviceIdType.MESH
BF16, F32 = jnp.bfloat16, jnp.float32
NEG = -1e30
R = 8
ORDER = (4, 3, 5, 2, 6, 1, 7)
GROUPS = 2
NH = 4 // GROUPS
KINDS = (0, 1)
ROWS1 = NH * 64 + 16
PIECE = NH * 8
PARTS = 64 // PIECE
ROWS2 = PIECE + 16


def dot(a, b):
    return jnp.dot(a, b, preferred_element_type=F32)


def pack_stats(top, low, rest):
    return jnp.concatenate([jnp.where(lax.broadcasted_iota(jnp.int32, (8, 128), 1) < 64, top, low), rest], 0)


def split3(x):
    hi = x.astype(BF16).astype(F32)
    mid = (x - hi).astype(BF16).astype(F32)
    return hi, mid, (x - hi) - mid


def unpack_stats(block):
    block = block.astype(F32)
    first = block[:8]
    other = pltpu.roll(first, 64, 1)
    lane = lax.broadcasted_iota(jnp.int32, (8, 128), 1)
    hi = jnp.where(lane < 64, first, other)
    mid = jnp.where(lane < 64, other, first)
    return hi + (mid + block[8:])


def kernel(
    q_hbm, k_hbm, v_hbm, vert_hbm, slash_hbm, w_hbm, o_ref,
    q_in, vert_in, slash_in, k_in, v_ext, w_ref, ktx, tri, qbuf, score, prob, stat,
    snd1, rcv1, snd2, rcv2, wcol, attn, proj, snd3, rcv3,
    load_sem, send_sem, recv_sem,
):
    ctx, hd = lax.axis_index("ctx"), lax.axis_index("head")
    z, y = ctx // R, ctx % R
    heads = q_in.shape[1] // 128

    def along(axis, k):
        return {"ctx": z * R + (y + k) % R} if axis == 0 else {"ctx": (z + k) % R * R + y}

    def place(axis):
        return y if axis == 0 else z

    loads = [
        pltpu.make_async_copy(src, dst, load_sem.at[i])
        for i, (src, dst) in enumerate(
            [
                (q_hbm, q_in),
                (vert_hbm, vert_in),
                (slash_hbm, slash_in),
                (k_hbm, k_in),
                (v_hbm, v_ext.at[:, pl.ds(0, 128)]),
                (w_hbm, w_ref),
            ]
        )
    ]
    for copy in loads:
        copy.start()
    barrier = pltpu.get_barrier_semaphore()
    for k in ORDER:
        for axis in (0, 1):
            pl.semaphore_signal(barrier, inc=1, device_id=along(axis, k), device_id_type=MESH)
        pl.semaphore_signal(barrier, inc=1, device_id={"head": (hd + k) % R}, device_id_type=MESH)

    loads[0].wait()
    for h in range(heads):
        qbuf[h, z, y] = q_in[:, h * 128 : (h + 1) * 128]

    pl.semaphore_wait(barrier, 3 * (R - 1))

    def send(src, dst, slot, device):
        copy = pltpu.make_async_remote_copy(
            src_ref=src, dst_ref=dst, send_sem=send_sem.at[slot], recv_sem=recv_sem.at[slot],
            device_id=device, device_id_type=MESH,
        )
        copy.start()

    pending = []

    def arrived(like, slot):
        copy = pltpu.make_async_remote_copy(
            src_ref=like, dst_ref=like, send_sem=send_sem.at[slot], recv_sem=recv_sem.at[slot],
            device_id=along(0, 1), device_id_type=MESH,
        )
        copy.wait_recv()
        pending.append(copy)

    def slot(phase, kind, group):
        return (phase * 2 + kind) * 4 + group

    def q1_send():
        for k in ORDER:
            for kind in KINDS:
                ref = qbuf.at[pl.ds(4 * kind, 4), z, y]
                send(ref, ref, slot(0, kind, 0), along(kind, k))

    def q1_wait():
        for kind in KINDS:
            arrived(qbuf.at[pl.ds(4 * kind, 4), 0, pl.ds(0, R - 1)], slot(0, kind, 0))

    def spread(axis, sign, block, direct, final):
        ref = block(place(axis))
        for k, where in ((-3 * sign, direct), (2 * sign, direct), (1, final), (-1, final)):
            send(ref, ref, where, along(axis, k % R))

    def relay(axis, sign, block, direct, final, like):
        arrived(like, direct)
        three, two = block((place(axis) + 3 * sign + R) % R), block((place(axis) - 2 * sign + R) % R)
        for ref, k in ((three, 1), (three, -1), (two, sign)):
            send(ref, ref, final, along(axis, k % R))

    def q_block(kind, pair):
        h = 4 * kind + pair
        return lambda o: qbuf.at[h, o] if kind == 0 else qbuf.at[h, :, o]

    def q2_send(pair):
        for kind in KINDS:
            spread(1 - kind, 1 - pair % 2 * 2, q_block(kind, pair), slot(1, kind, pair), slot(2, kind, pair))

    def q2_relay(pair):
        for kind in KINDS:
            like = qbuf.at[4 * kind + pair, pl.ds(0, 2)]
            relay(1 - kind, 1 - pair % 2 * 2, q_block(kind, pair), slot(1, kind, pair), slot(2, kind, pair), like)

    def q2_wait(pair):
        for kind in KINDS:
            arrived(qbuf.at[4 * kind + pair, pl.ds(0, 5)], slot(2, kind, pair))

    lane = lax.broadcasted_iota(jnp.int32, (8, 128), 1)
    sub = lax.broadcasted_iota(jnp.int32, (8, 128), 0)
    scale = math.log2(math.e) / math.sqrt(128.0)

    def prepare():
        for copy in loads[1:]:
            copy.wait()
        v_ext[:, 128:] = jnp.ones((v_ext.shape[0], 128), BF16)
        stat[...] = jnp.zeros_like(stat)
        kt = k_in[...].astype(F32).T.astype(BF16)
        for h in range(heads):
            ktx[h, :128, :] = kt

    def prepare_masks():
        first = 508 - 8 * ctx
        vert, slash = vert_in[...], slash_in[...]
        by_slash = {
            d: jnp.max(jnp.where(slash == first + d, 1.0, 0.0), axis=1, keepdims=True) for d in range(-7, 4)
        }
        by_vert = [jnp.max(jnp.where(vert == 8 * ctx + j, 1.0, 0.0), axis=1, keepdims=True) for j in range(8)]
        masks = []
        for b in range(4):
            blocks = []
            for j in range(8):
                hit = jnp.maximum(by_slash[b - j], by_vert[j])
                row = jnp.broadcast_to(jnp.where(hit > 0.5, 0.0, NEG), (heads, 128))
                if j > b + 4:
                    row = jnp.where(ctx == R * R - 1, NEG, row)
                blocks.append(row)
            masks.append(jnp.concatenate(blocks, 1))
        local = masks[0].shape[1]
        for h in range(heads):
            rows = [mask[h : h + 1, :] for mask in masks] + [jnp.zeros((124, local), F32)]
            ktx[h, 128:, :] = jnp.concatenate(rows, 0).astype(BF16)
        r128 = lax.broadcasted_iota(jnp.int32, (128, 128), 0)
        c128 = lax.broadcasted_iota(jnp.int32, (128, 128), 1)
        tri[...] = jnp.where((c128 <= r128) | (ctx != R * R - 1), 0.0, NEG)

    def scores(kind, pair):
        row = lax.broadcasted_iota(jnp.int32, (512, 128), 0) // 128
        chooser = jnp.where(lax.broadcasted_iota(jnp.int32, (512, 128), 1) == row, 1.0, 0.0).astype(BF16)
        h = 4 * kind + pair
        score[kind] = dot(jnp.concatenate([qbuf[h].reshape(512, 128), chooser], 1), ktx[h])

    def weigh(kind):
        tops = []
        for b in range(4):
            rows = slice(b * 128, (b + 1) * 128)
            c = (4 + b) * 128
            s = score[kind, rows]
            parts = [s[:, :c], s[:, c : c + 128] + tri[...]] + ([s[:, c + 128 :]] if b < 3 else [])
            s = jnp.concatenate(parts, axis=1)
            top = jnp.max(s, axis=1, keepdims=True) * scale
            prob[kind, rows] = jnp.exp2(s * scale - top).astype(BF16)
            tops.append(top)
        return tops

    def finish(kind, pair, tops):
        group, hh = pair // NH, pair % NH
        for b in range(4):
            rows = slice(b * 128, (b + 1) * 128)
            out = dot(prob[kind, rows], v_ext[...])
            total = out[:, 128:]
            mean = (out[:, :128] / total).astype(BF16)
            snd1[kind, group, 2 * b : 2 * b + 2, hh * 64 : (hh + 1) * 64, :] = mean.reshape(2, 64, 128)
            at = lax.broadcasted_iota(jnp.int32, (128, 128), 1)
            stat[kind, rows] = jnp.where(at == hh, tops[b] + jnp.log2(total), stat[kind, rows])

    def attend(pair):
        scores(0, pair)
        tops0 = weigh(0)
        scores(1, pair)
        finish(0, pair, tops0)
        tops1 = weigh(1)
        finish(1, pair, tops1)

    def statistics(kind, group):
        for b in range(4):
            block = stat[kind, b * 128 : (b + 1) * 128, :].T[:8]
            hi, mid, lo = split3(block)
            turned = [pltpu.roll(x, 64, 1) for x in (hi, mid, lo)]
            even = pack_stats(hi, turned[1], jnp.where(lane < 64, lo, turned[2]))
            odd = pack_stats(turned[0], mid, jnp.where(lane < 64, turned[2], lo))
            snd1[kind, group, 2 * b, NH * 64 :, :] = even.astype(BF16)
            snd1[kind, group, 2 * b + 1, NH * 64 :, :] = odd.astype(BF16)

    def r1_rows(pair):
        hh = pair % NH
        return pl.ds(hh * 64, 64 if hh < NH - 1 else 64 + 16)

    def r1_send(kind, pair):
        group, rows = pair // NH, r1_rows(pair)
        for k in ORDER:
            src, dst = snd1.at[kind, group, (place(kind) + k) % R, rows], rcv1.at[kind, group, k - 1, rows]
            send(src, dst, slot(3, kind, pair), along(kind, k))

    def r1_combine(kind, group):
        for pair in range(group * NH, (group + 1) * NH):
            arrived(rcv1.at[kind, group, :, r1_rows(pair)], slot(3, kind, pair))
        own = snd1.at[kind, group, place(kind)]
        refs = [own] + [rcv1.at[kind, group, k] for k in range(R - 1)]
        logs = [unpack_stats(ref[NH * 64 :, :]) for ref in refs]
        top = functools.reduce(jnp.maximum, logs)
        raised = [jnp.exp2(x - top) for x in logs]
        total = functools.reduce(jnp.add, raised)
        cols = jnp.concatenate([x / total for x in raised] + [jnp.zeros((64, 128), F32)], 0).T
        for hh in range(NH):
            acc = None
            for s, ref in enumerate(refs):
                term = cols[:64, s * 8 + hh : s * 8 + hh + 1] * ref[hh * 64 : (hh + 1) * 64, :].astype(F32)
                acc = term if acc is None else acc + term
            acc = acc.astype(BF16).reshape(PARTS, PIECE, 128)
            snd2[kind, group, hh * PARTS : (hh + 1) * PARTS, :PIECE, :] = acc
        hi, mid, lo = split3(top + jnp.log2(total))
        packed = pack_stats(hi, mid, lo).astype(BF16)
        for to in range(R):
            snd2[kind, group, to, PIECE:, :] = packed

    def r2_send(kind, group):
        axis = 1 - kind
        for k in ORDER:
            to = (place(axis) + k) % R
            send(snd2.at[kind, group, to], rcv2.at[kind, group, k - 1], slot(4, kind, group), along(axis, k))

    def own_piece(kind, group):
        axis = 1 - kind
        me = place(axis)
        start = pl.multiple_of(me % PARTS * PIECE, PIECE)
        return attn.at[kind, group, place(kind), me // PARTS, pl.ds(start, PIECE)]

    def r2_combine(kind, group):
        arrived(rcv2.at[kind, group], slot(4, kind, group))
        me = place(1 - kind)
        hh, part = me // PARTS, me % PARTS
        refs = [snd2.at[kind, group, me]] + [rcv2.at[kind, group, k] for k in range(R - 1)]
        logs = jnp.zeros((8, 128), F32)
        for s, ref in enumerate(refs):
            row = jnp.sum(jnp.where(sub == hh, unpack_stats(ref[PIECE:, :]), 0.0), axis=0, keepdims=True)
            logs = jnp.where(sub == s, row, logs)
        raised = jnp.exp2(logs - jnp.max(logs, axis=0, keepdims=True))
        weight = raised / jnp.sum(raised, axis=0, keepdims=True)
        wcol[...] = jnp.concatenate([weight, jnp.zeros((120, 128), F32)], 0).T
        cols = wcol[pl.ds(pl.multiple_of(part * PIECE, PIECE), PIECE), :]
        acc = None
        for s, ref in enumerate(refs):
            term = cols[:, s : s + 1] * ref[:PIECE, :].astype(F32)
            acc = term if acc is None else acc + term
        own_piece(kind, group)[...] = acc.astype(BF16)

    def g1_send(kind, group):
        for k in ORDER:
            ref = own_piece(kind, group)
            send(ref, ref, slot(5, kind, group), along(1 - kind, k))

    def g1_wait(kind, group):
        arrived(rcv2.at[kind, group, :, pl.ds(0, PIECE)], slot(5, kind, group))

    def g2_block(kind, group):
        return lambda o: attn.at[kind, group, o]

    def g2_send(kind, group):
        ref = attn.at[kind, group, place(kind)]
        for k in ORDER:
            send(ref, ref, slot(6, kind, group), along(kind, k))

    def g2_wait(kind, group):
        arrived(attn.at[kind, group, pl.ds(0, R - 1)], slot(6, kind, group))

    def project(kind, group):
        acc = None
        for hh in range(0, NH, 2):
            left = [attn[kind, group, :, hh + i].reshape(512, 128) for i in range(2)]
            row = (kind * 4 + group * NH + hh) * 128
            term = dot(jnp.concatenate(left, 1), w_ref[row : row + 256, :])
            acc = term if acc is None else acc + term
        return acc

    def tail():
        total = None
        for group in range(GROUPS):
            for kind in KINDS:
                g2_wait(kind, group)
                term = project(kind, group)
                total = term if total is None else total + term
        proj[...] = total
        snd3[...] = total.astype(BF16).reshape(R, 64, 128)
        last = slot(8, 0, 0)
        for k in ORDER:
            to = (hd + k) % R
            send(snd3.at[to], rcv3.at[k - 1], last, {"head": to})
        arrived(rcv3, last)
        out = proj[pl.ds(pl.multiple_of(hd * 64, 64), 64), :]
        for k in range(R - 1):
            out = out + rcv3[k].astype(F32)
        o_ref[...] = out.astype(BF16)

    steps = [(q1_send,), (prepare,), (q1_wait,)]
    steps += [(q2_send, pair) for pair in range(4)] + [(prepare_masks,)]
    steps += [(q2_relay, pair) for pair in range(3)]
    for pair in range(4):
        steps += [(q2_wait, pair), (attend, pair)]
        for kind in KINDS:
            if pair % NH == NH - 1:
                steps += [(statistics, kind, pair // NH)]
            steps += [(r1_send, kind, pair)]
        if pair == 0:
            steps += [(q2_relay, 3)]
    both = [(kind, group) for group in range(GROUPS) for kind in KINDS]
    for first, second in ((r1_combine, r2_send), (r2_combine, g1_send), (g1_wait, g2_send)):
        for args in both:
            steps += [(first, *args), (second, *args)]
    steps += [(tail,)]
    for step, *args in steps:
        step(*args)
    for copy in pending:
        copy.wait_send()


def body(queries, cache_keys, cache_values, vertical_blocks, slash_offsets, out_weight):
    keys, values = cache_keys[:, 0, :], cache_values[:, 0, :]
    local, width = keys.shape
    heads = vertical_blocks.shape[0]
    slots = 8 * 2 * 4 + 1
    vmem, hbm = pl.BlockSpec(memory_space=pltpu.VMEM), pl.BlockSpec(memory_space=pltpu.HBM)
    return pl.pallas_call(
        kernel,
        out_shape=jax.ShapeDtypeStruct((64, 128), BF16),
        in_specs=[hbm] * 6,
        out_specs=vmem,
        scratch_shapes=[
            pltpu.VMEM(queries.shape, BF16),
            pltpu.VMEM(vertical_blocks.shape, jnp.int32),
            pltpu.VMEM(slash_offsets.shape, jnp.int32),
            pltpu.VMEM((local, width), BF16),
            pltpu.VMEM((local, 256), BF16),
            pltpu.VMEM(out_weight.shape, BF16),
            pltpu.VMEM((heads, 2 * width, local), BF16),
            pltpu.VMEM((128, 128), F32),
            pltpu.VMEM((heads, R, R, 8, 128), BF16),
            pltpu.VMEM((2, 512, local), F32),
            pltpu.VMEM((2, 512, local), BF16),
            pltpu.VMEM((2, 512, 128), F32),
            pltpu.VMEM((2, GROUPS, R, ROWS1, 128), BF16),
            pltpu.VMEM((2, GROUPS, R - 1, ROWS1, 128), BF16),
            pltpu.VMEM((2, GROUPS, R, ROWS2, 128), BF16),
            pltpu.VMEM((2, GROUPS, R - 1, ROWS2, 128), BF16),
            pltpu.VMEM((128, 128), F32),
            pltpu.VMEM((2, GROUPS, R, NH, 64, 128), BF16),
            pltpu.VMEM((512, 128), F32),
            pltpu.VMEM((R, 64, 128), BF16),
            pltpu.VMEM((R - 1, 64, 128), BF16),
            pltpu.SemaphoreType.DMA((6,)),
            pltpu.SemaphoreType.DMA((slots,)),
            pltpu.SemaphoreType.DMA((slots,)),
        ],
        compiler_params=pltpu.CompilerParams(
            collective_id=0, has_side_effects=True, vmem_limit_bytes=61 * 1024 * 1024
        ),
    )(queries, keys, values, vertical_blocks, slash_offsets, out_weight)


def solution(mesh):
    return jax.shard_map(
        body,
        mesh=mesh,
        in_specs=(
            P("ctx", "head"),
            P("ctx", "head", None),
            P("ctx", "head", None),
            P("head", None),
            P("head", None),
            P("head", "ctx"),
        ),
        out_specs=P("head", "ctx"),
        check_vma=False,
    )
```

```python
import functools
import math

import jax
import jax.numpy as jnp
from jax import lax
from jax.experimental import pallas as pl
from jax.experimental.pallas import tpu as pltpu
from jax.sharding import PartitionSpec as P

MESH = pl.DeviceIdType.MESH
BF16, F32 = jnp.bfloat16, jnp.float32
NEG = -1e30
R = 8
ORDER = (4, 3, 5, 2, 6, 1, 7)
GROUPS = 2
NH = 4 // GROUPS
KINDS = (0, 1)
ROWS1 = NH * 64 + 16
PIECE = NH * 8
PARTS = 64 // PIECE
ROWS2 = PIECE + 16


def dot(a, b):
    return jnp.dot(a, b, preferred_element_type=F32)


def pack_stats(top, low, rest):
    return jnp.concatenate([jnp.where(lax.broadcasted_iota(jnp.int32, (8, 128), 1) < 64, top, low), rest], 0)


def split3(x):
    hi = x.astype(BF16).astype(F32)
    mid = (x - hi).astype(BF16).astype(F32)
    return hi, mid, (x - hi) - mid


def unpack_stats(block):
    block = block.astype(F32)
    first = block[:8]
    other = pltpu.roll(first, 64, 1)
    lane = lax.broadcasted_iota(jnp.int32, (8, 128), 1)
    hi = jnp.where(lane < 64, first, other)
    mid = jnp.where(lane < 64, other, first)
    return hi + (mid + block[8:])


def kernel(
    q_hbm, k_hbm, v_hbm, vert_hbm, slash_hbm, w_hbm, o_ref,
    q_in, vert_in, slash_in, k_in, v_ext, w_ref, ktx, tri, qbuf, score, prob, stat,
    snd1, rcv1, snd2, rcv2, wcol, attn, proj, snd3, rcv3,
    load_sem, send_sem, recv_sem,
):
    ctx, hd = lax.axis_index("ctx"), lax.axis_index("head")
    z, y = ctx // R, ctx % R
    heads = q_in.shape[1] // 128

    def along(axis, k):
        return {"ctx": z * R + (y + k) % R} if axis == 0 else {"ctx": (z + k) % R * R + y}

    def place(axis):
        return y if axis == 0 else z

    loads = [
        pltpu.make_async_copy(src, dst, load_sem.at[i])
        for i, (src, dst) in enumerate(
            [
                (q_hbm, q_in),
                (vert_hbm, vert_in),
                (slash_hbm, slash_in),
                (k_hbm, k_in),
                (v_hbm, v_ext.at[:, pl.ds(0, 128)]),
                (w_hbm, w_ref),
            ]
        )
    ]
    for copy in loads:
        copy.start()
    barrier = pltpu.get_barrier_semaphore()
    for k in ORDER:
        for axis in (0, 1):
            pl.semaphore_signal(barrier, inc=1, device_id=along(axis, k), device_id_type=MESH)
        pl.semaphore_signal(barrier, inc=1, device_id={"head": (hd + k) % R}, device_id_type=MESH)

    loads[0].wait()
    for h in range(heads):
        qbuf[h, z, y] = q_in[:, h * 128 : (h + 1) * 128]

    pl.semaphore_wait(barrier, 3 * (R - 1))

    def send(src, dst, slot, device):
        copy = pltpu.make_async_remote_copy(
            src_ref=src, dst_ref=dst, send_sem=send_sem.at[slot], recv_sem=recv_sem.at[slot],
            device_id=device, device_id_type=MESH,
        )
        copy.start()

    pending = []

    def arrived(like, slot):
        copy = pltpu.make_async_remote_copy(
            src_ref=like, dst_ref=like, send_sem=send_sem.at[slot], recv_sem=recv_sem.at[slot],
            device_id=along(0, 1), device_id_type=MESH,
        )
        copy.wait_recv()
        pending.append(copy)

    def slot(phase, kind, group):
        return (phase * 2 + kind) * 4 + group

    def q1_send():
        for k in ORDER:
            for kind in KINDS:
                ref = qbuf.at[pl.ds(4 * kind, 4), z, y]
                send(ref, ref, slot(0, kind, 0), along(kind, k))

    def q1_wait():
        for kind in KINDS:
            arrived(qbuf.at[pl.ds(4 * kind, 4), 0, pl.ds(0, R - 1)], slot(0, kind, 0))

    def spread(axis, sign, block, direct, final):
        ref = block(place(axis))
        for k, where in ((-3 * sign, direct), (2 * sign, direct), (1, final), (-1, final)):
            send(ref, ref, where, along(axis, k % R))

    def relay(axis, sign, block, direct, final, like):
        arrived(like, direct)
        three, two = block((place(axis) + 3 * sign + R) % R), block((place(axis) - 2 * sign + R) % R)
        for ref, k in ((three, 1), (three, -1), (two, sign)):
            send(ref, ref, final, along(axis, k % R))

    def q_block(kind, pair):
        h = 4 * kind + pair
        return lambda o: qbuf.at[h, o] if kind == 0 else qbuf.at[h, :, o]

    def q2_send(pair):
        for kind in KINDS:
            spread(1 - kind, 1 - pair % 2 * 2, q_block(kind, pair), slot(1, kind, pair), slot(2, kind, pair))

    def q2_relay(pair):
        for kind in KINDS:
            like = qbuf.at[4 * kind + pair, pl.ds(0, 2)]
            relay(1 - kind, 1 - pair % 2 * 2, q_block(kind, pair), slot(1, kind, pair), slot(2, kind, pair), like)

    def q2_wait(pair):
        for kind in KINDS:
            arrived(qbuf.at[4 * kind + pair, pl.ds(0, 5)], slot(2, kind, pair))

    lane = lax.broadcasted_iota(jnp.int32, (8, 128), 1)
    sub = lax.broadcasted_iota(jnp.int32, (8, 128), 0)
    scale = math.log2(math.e) / math.sqrt(128.0)

    def prepare():
        for copy in loads[1:]:
            copy.wait()
        v_ext[:, 128:] = jnp.ones((v_ext.shape[0], 128), BF16)
        stat[...] = jnp.zeros_like(stat)
        kt = k_in[...].astype(F32).T.astype(BF16)
        for h in range(heads):
            ktx[h, :128, :] = kt

    def prepare_masks():
        first = 508 - 8 * ctx
        vert, slash = vert_in[...], slash_in[...]
        by_slash = {
            d: jnp.max(jnp.where(slash == first + d, 1.0, 0.0), axis=1, keepdims=True) for d in range(-7, 4)
        }
        by_vert = [jnp.max(jnp.where(vert == 8 * ctx + j, 1.0, 0.0), axis=1, keepdims=True) for j in range(8)]
        masks = []
        for b in range(4):
            blocks = []
            for j in range(8):
                hit = jnp.maximum(by_slash[b - j], by_vert[j])
                row = jnp.broadcast_to(jnp.where(hit > 0.5, 0.0, NEG), (heads, 128))
                if j > b + 4:
                    row = jnp.where(ctx == R * R - 1, NEG, row)
                blocks.append(row)
            masks.append(jnp.concatenate(blocks, 1))
        local = masks[0].shape[1]
        for h in range(heads):
            rows = [mask[h : h + 1, :] for mask in masks] + [jnp.zeros((124, local), F32)]
            ktx[h, 128:, :] = jnp.concatenate(rows, 0).astype(BF16)
        r128 = lax.broadcasted_iota(jnp.int32, (128, 128), 0)
        c128 = lax.broadcasted_iota(jnp.int32, (128, 128), 1)
        tri[...] = jnp.where((c128 <= r128) | (ctx != R * R - 1), 0.0, NEG)

    def scores(kind, pair):
        row = lax.broadcasted_iota(jnp.int32, (512, 128), 0) // 128
        chooser = jnp.where(lax.broadcasted_iota(jnp.int32, (512, 128), 1) == row, 1.0, 0.0).astype(BF16)
        h = 4 * kind + pair
        score[kind] = dot(jnp.concatenate([qbuf[h].reshape(512, 128), chooser], 1), ktx[h])

    def weigh(kind):
        tops = []
        for b in range(4):
            rows = slice(b * 128, (b + 1) * 128)
            c = (4 + b) * 128
            s = score[kind, rows]
            parts = [s[:, :c], s[:, c : c + 128] + tri[...]] + ([s[:, c + 128 :]] if b < 3 else [])
            s = jnp.concatenate(parts, axis=1)
            top = jnp.max(s, axis=1, keepdims=True) * scale
            prob[kind, rows] = jnp.exp2(s * scale - top).astype(BF16)
            tops.append(top)
        return tops

    def finish(kind, pair, tops):
        group, hh = pair // NH, pair % NH
        for b in range(4):
            rows = slice(b * 128, (b + 1) * 128)
            out = dot(prob[kind, rows], v_ext[...])
            total = out[:, 128:]
            mean = (out[:, :128] / total).astype(BF16)
            snd1[kind, group, 2 * b : 2 * b + 2, hh * 64 : (hh + 1) * 64, :] = mean.reshape(2, 64, 128)
            at = lax.broadcasted_iota(jnp.int32, (128, 128), 1)
            stat[kind, rows] = jnp.where(at == hh, tops[b] + jnp.log2(total), stat[kind, rows])

    def attend(pair):
        scores(0, pair)
        tops0 = weigh(0)
        scores(1, pair)
        finish(0, pair, tops0)
        tops1 = weigh(1)
        finish(1, pair, tops1)

    def statistics(kind, group):
        for b in range(4):
            block = stat[kind, b * 128 : (b + 1) * 128, :].T[:8]
            hi, mid, lo = split3(block)
            turned = [pltpu.roll(x, 64, 1) for x in (hi, mid, lo)]
            even = pack_stats(hi, turned[1], jnp.where(lane < 64, lo, turned[2]))
            odd = pack_stats(turned[0], mid, jnp.where(lane < 64, turned[2], lo))
            snd1[kind, group, 2 * b, NH * 64 :, :] = even.astype(BF16)
            snd1[kind, group, 2 * b + 1, NH * 64 :, :] = odd.astype(BF16)

    def r1_rows(pair):
        hh = pair % NH
        if pair < 4 - NH:
            return pl.ds(0, ROWS1) if hh == NH - 1 else None
        return pl.ds(hh * 64, 64 if hh < NH - 1 else 64 + 16)

    def r1_send(kind, pair):
        group, rows = pair // NH, r1_rows(pair)
        for k in ORDER:
            src, dst = snd1.at[kind, group, (place(kind) + k) % R, rows], rcv1.at[kind, group, k - 1, rows]
            send(src, dst, slot(3, kind, pair), along(kind, k))

    def r1_combine(kind, group):
        for pair in range(group * NH, (group + 1) * NH):
            if r1_rows(pair) is None:
                continue
            arrived(rcv1.at[kind, group, :, r1_rows(pair)], slot(3, kind, pair))
        own = snd1.at[kind, group, place(kind)]
        refs = [own] + [rcv1.at[kind, group, k] for k in range(R - 1)]
        logs = [unpack_stats(ref[NH * 64 :, :]) for ref in refs]
        top = functools.reduce(jnp.maximum, logs)
        raised = [jnp.exp2(x - top) for x in logs]
        total = functools.reduce(jnp.add, raised)
        cols = jnp.concatenate([x / total for x in raised] + [jnp.zeros((64, 128), F32)], 0).T
        for hh in range(NH):
            acc = None
            for s, ref in enumerate(refs):
                term = cols[:64, s * 8 + hh : s * 8 + hh + 1] * ref[hh * 64 : (hh + 1) * 64, :].astype(F32)
                acc = term if acc is None else acc + term
            acc = acc.astype(BF16).reshape(PARTS, PIECE, 128)
            snd2[kind, group, hh * PARTS : (hh + 1) * PARTS, :PIECE, :] = acc
        hi, mid, lo = split3(top + jnp.log2(total))
        packed = pack_stats(hi, mid, lo).astype(BF16)
        for to in range(R):
            snd2[kind, group, to, PIECE:, :] = packed

    def r2_send(kind, group):
        axis = 1 - kind
        for k in ORDER:
            to = (place(axis) + k) % R
            send(snd2.at[kind, group, to], rcv2.at[kind, group, k - 1], slot(4, kind, group), along(axis, k))

    def own_piece(kind, group):
        axis = 1 - kind
        me = place(axis)
        start = pl.multiple_of(me % PARTS * PIECE, PIECE)
        return attn.at[kind, group, place(kind), me // PARTS, pl.ds(start, PIECE)]

    def r2_combine(kind, group):
        arrived(rcv2.at[kind, group], slot(4, kind, group))
        me = place(1 - kind)
        hh, part = me // PARTS, me % PARTS
        refs = [snd2.at[kind, group, me]] + [rcv2.at[kind, group, k] for k in range(R - 1)]
        logs = jnp.zeros((8, 128), F32)
        for s, ref in enumerate(refs):
            row = jnp.sum(jnp.where(sub == hh, unpack_stats(ref[PIECE:, :]), 0.0), axis=0, keepdims=True)
            logs = jnp.where(sub == s, row, logs)
        raised = jnp.exp2(logs - jnp.max(logs, axis=0, keepdims=True))
        weight = raised / jnp.sum(raised, axis=0, keepdims=True)
        wcol[...] = jnp.concatenate([weight, jnp.zeros((120, 128), F32)], 0).T
        cols = wcol[pl.ds(pl.multiple_of(part * PIECE, PIECE), PIECE), :]
        acc = None
        for s, ref in enumerate(refs):
            term = cols[:, s : s + 1] * ref[:PIECE, :].astype(F32)
            acc = term if acc is None else acc + term
        own_piece(kind, group)[...] = acc.astype(BF16)

    def g1_send(kind, group):
        for k in ORDER:
            ref = own_piece(kind, group)
            send(ref, ref, slot(5, kind, group), along(1 - kind, k))

    def g1_wait(kind, group):
        arrived(rcv2.at[kind, group, :, pl.ds(0, PIECE)], slot(5, kind, group))

    def g2_block(kind, group):
        return lambda o: attn.at[kind, group, o]

    def g2_send(kind, group):
        ref = attn.at[kind, group, place(kind)]
        for k in ORDER:
            send(ref, ref, slot(6, kind, group), along(kind, k))

    def g2_wait(kind, group):
        arrived(attn.at[kind, group, pl.ds(0, R - 1)], slot(6, kind, group))

    def project(kind, group):
        acc = None
        for hh in range(0, NH, 2):
            left = [attn[kind, group, :, hh + i].reshape(512, 128) for i in range(2)]
            row = (kind * 4 + group * NH + hh) * 128
            term = dot(jnp.concatenate(left, 1), w_ref[row : row + 256, :])
            acc = term if acc is None else acc + term
        return acc

    def tail():
        total = None
        for group in range(GROUPS):
            for kind in KINDS:
                g2_wait(kind, group)
                term = project(kind, group)
                total = term if total is None else total + term
        proj[...] = total
        snd3[...] = total.astype(BF16).reshape(R, 64, 128)
        last = slot(8, 0, 0)
        for k in ORDER:
            to = (hd + k) % R
            send(snd3.at[to], rcv3.at[k - 1], last, {"head": to})
        arrived(rcv3, last)
        out = proj[pl.ds(pl.multiple_of(hd * 64, 64), 64), :]
        for k in range(R - 1):
            out = out + rcv3[k].astype(F32)
        o_ref[...] = out.astype(BF16)

    steps = [(q1_send,), (prepare,), (q1_wait,)]
    steps += [(q2_send, pair) for pair in range(4)] + [(prepare_masks,)]
    steps += [(q2_relay, pair) for pair in range(3)]
    for pair in range(4):
        steps += [(q2_wait, pair), (attend, pair)]
        for kind in KINDS:
            if pair % NH == NH - 1:
                steps += [(statistics, kind, pair // NH)]
            if r1_rows(pair) is not None:
                steps += [(r1_send, kind, pair)]
        if pair == 0:
            steps += [(q2_relay, 3)]
    both = [(kind, group) for group in range(GROUPS) for kind in KINDS]
    for first, second in ((r1_combine, r2_send), (r2_combine, g1_send), (g1_wait, g2_send)):
        for args in both:
            steps += [(first, *args), (second, *args)]
    steps += [(tail,)]
    for step, *args in steps:
        step(*args)
    for copy in pending:
        copy.wait_send()


def body(queries, cache_keys, cache_values, vertical_blocks, slash_offsets, out_weight):
    keys, values = cache_keys[:, 0, :], cache_values[:, 0, :]
    local, width = keys.shape
    heads = vertical_blocks.shape[0]
    slots = 8 * 2 * 4 + 1
    vmem, hbm = pl.BlockSpec(memory_space=pltpu.VMEM), pl.BlockSpec(memory_space=pltpu.HBM)
    return pl.pallas_call(
        kernel,
        out_shape=jax.ShapeDtypeStruct((64, 128), BF16),
        in_specs=[hbm] * 6,
        out_specs=vmem,
        scratch_shapes=[
            pltpu.VMEM(queries.shape, BF16),
            pltpu.VMEM(vertical_blocks.shape, jnp.int32),
            pltpu.VMEM(slash_offsets.shape, jnp.int32),
            pltpu.VMEM((local, width), BF16),
            pltpu.VMEM((local, 256), BF16),
            pltpu.VMEM(out_weight.shape, BF16),
            pltpu.VMEM((heads, 2 * width, local), BF16),
            pltpu.VMEM((128, 128), F32),
            pltpu.VMEM((heads, R, R, 8, 128), BF16),
            pltpu.VMEM((2, 512, local), F32),
            pltpu.VMEM((2, 512, local), BF16),
            pltpu.VMEM((2, 512, 128), F32),
            pltpu.VMEM((2, GROUPS, R, ROWS1, 128), BF16),
            pltpu.VMEM((2, GROUPS, R - 1, ROWS1, 128), BF16),
            pltpu.VMEM((2, GROUPS, R, ROWS2, 128), BF16),
            pltpu.VMEM((2, GROUPS, R - 1, ROWS2, 128), BF16),
            pltpu.VMEM((128, 128), F32),
            pltpu.VMEM((2, GROUPS, R, NH, 64, 128), BF16),
            pltpu.VMEM((512, 128), F32),
            pltpu.VMEM((R, 64, 128), BF16),
            pltpu.VMEM((R - 1, 64, 128), BF16),
            pltpu.SemaphoreType.DMA((6,)),
            pltpu.SemaphoreType.DMA((slots,)),
            pltpu.SemaphoreType.DMA((slots,)),
        ],
        compiler_params=pltpu.CompilerParams(
            collective_id=0, has_side_effects=True, vmem_limit_bytes=61 * 1024 * 1024
        ),
    )(queries, keys, values, vertical_blocks, slash_offsets, out_weight)


def solution(mesh):
    return jax.shard_map(
        body,
        mesh=mesh,
        in_specs=(
            P("ctx", "head"),
            P("ctx", "head", None),
            P("ctx", "head", None),
            P("head", None),
            P("head", None),
            P("head", "ctx"),
        ),
        out_specs=P("head", "ctx"),
        check_vma=False,
    )
```
